32 devices in a mesh: fsdp: 32 (over z, y, x, core).
Axes of the slice: x: 2, y: 2, z: 4, core: 2. Of those that a mesh axis runs over, the one named last changes fastest.
Arguments:
- tokens: bfloat16 [8192, 1536], P('fsdp'), may hold values from -6 to 6
- norm1_gain: bfloat16 [1536], P('fsdp'), may hold values from 0.5 to 1.5
- w_query: bfloat16 [1536, 1536], P('fsdp'), may hold values from -0.15625 to 0.15625
- w_key: bfloat16 [1536, 768], P('fsdp'), may hold values from -0.15625 to 0.15625
- w_value: bfloat16 [1536, 768], P('fsdp'), may hold values from -0.15625 to 0.15625
- w_out: bfloat16 [1536, 1536], P('fsdp'), may hold values from -1.25 to 1.25
- norm2_gain: bfloat16 [1536], P('fsdp'), may hold values from 0.5 to 1.5
- w_gate: bfloat16 [1536, 4096], P('fsdp'), may hold values from -0.15625 to 0.15625
- w_up: bfloat16 [1536, 4096], P('fsdp'), may hold values from -0.15625 to 0.15625
- w_down: bfloat16 [4096, 1536], P('fsdp'), may hold values from -0.09375 to 0.09375
- cotangent: bfloat16 [8192, 1536], P('fsdp'), may hold values from -6 to 6
Outputs:
- output: bfloat16 [8192, 1536], P('fsdp')
- grad_tokens: float32 [8192, 1536], P('fsdp')
- grad_norm1_gain: float32 [1536], P('fsdp')
- grad_w_query: float32 [1536, 1536], P('fsdp')
- grad_w_key: float32 [1536, 768], P('fsdp')
- grad_w_value: float32 [1536, 768], P('fsdp')
- grad_w_out: float32 [1536, 1536], P('fsdp')
- grad_norm2_gain: float32 [1536], P('fsdp')
- grad_w_gate: float32 [1536, 4096], P('fsdp')
- grad_w_up: float32 [1536, 4096], P('fsdp')
- grad_w_down: float32 [4096, 1536], P('fsdp')
The draws below stay inside these ranges and needn't reach their ends.
All inputs are finite; a program needn't handle non-finite values.
Results may differ from the reference program's by a relative error of at most 0.015.
Values may be sent and summed in bfloat16 or wider, within the bound.
A program may use at most 384 MiB of HBM per device.

```python
import math
from functools import partial
import jax
import jax.numpy as jnp
from jax import lax

D = 1536
HEADS = 16
KV_HEADS = 8
HEAD_DIM = 96
FF = 4096
SEQ = 256
TOKENS = 8192


def block_levels(own_key, extent, cuts, smallest, largest):
    def one(dim, blocks):
        steps = jax.random.uniform(jax.random.fold_in(jax.random.fold_in(own_key, 6), dim), (blocks,), jnp.float32, smallest / len(cuts), largest / len(cuts))
        return jnp.repeat(jnp.exp(steps), extent[dim] // blocks).reshape((-1,) + (1,) * (len(extent) - dim - 1))

    gain = one(*cuts[0])
    for cut in cuts[1:]:
        gain = gain * one(*cut)
    return gain


def scatter_about(rng, shape, scale, most, shards=(), held_as=jnp.bfloat16):
    values = scale * jax.random.normal(rng, shape, jnp.float32)
    if shards:
        values = values * block_levels(rng, shape, shards, -0.22, 0.18)
    return jnp.clip(values, -most, most).astype(held_as)


def setup_inputs(seed: int = 0) -> dict:
    key_of = jax.random.split(jax.random.key(seed), 12)
    tokens = scatter_about(key_of[0], (TOKENS, D), 1.0, 6.0, ((0, 32),))
    norm1_gain = jnp.clip(1.0 + 0.1 * jax.random.normal(key_of[1], (D,), jnp.float32), 0.5, 1.5).astype(jnp.bfloat16)
    w_query = scatter_about(key_of[2], (D, HEADS * HEAD_DIM), D ** -0.5, 0.15625, ((0, 32),))
    w_key = scatter_about(key_of[3], (D, KV_HEADS * HEAD_DIM), D ** -0.5, 0.15625, ((0, 32),))
    w_value = scatter_about(key_of[4], (D, KV_HEADS * HEAD_DIM), D ** -0.5, 0.15625, ((0, 32),))
    w_out = scatter_about(key_of[5], (HEADS * HEAD_DIM, D), (HEADS * HEAD_DIM // 64) ** -0.5, 1.25, ((0, 32),))
    norm2_gain = jnp.clip(1.0 + 0.1 * jax.random.normal(key_of[6], (D,), jnp.float32), 0.5, 1.5).astype(jnp.bfloat16)
    w_gate = scatter_about(key_of[7], (D, FF), D ** -0.5, 0.15625, ((0, 32),))
    w_up = scatter_about(key_of[8], (D, FF), D ** -0.5, 0.15625, ((0, 32),))
    w_down = scatter_about(key_of[9], (FF, D), FF ** -0.5, 0.09375, ((0, 32),))
    cotangent = scatter_about(key_of[10], (TOKENS, D), 1.0, 6.0, ((0, 32),))
    return dict(tokens=tokens, norm1_gain=norm1_gain, w_query=w_query, w_key=w_key, w_value=w_value, w_out=w_out, norm2_gain=norm2_gain, w_gate=w_gate, w_up=w_up, w_down=w_down, cotangent=cotangent)


EPSILON = 1e-05
THETA = 100000.0
HIGH = lax.Precision.HIGHEST

@jax.custom_vjp
def low(v):
    return lax.optimization_barrier(v.astype(jnp.bfloat16)).astype(jnp.float32)

@jax.custom_vjp
def low_back(v):
    return v

def low_keep(v):
    return (low(v), None)

def low_pass(kept, grad):
    return (grad,)

def back_keep(v):
    return (v, None)

def back_low(kept, grad):
    return (low(grad),)
low.defvjp(low_keep, low_pass)
low_back.defvjp(back_keep, back_low)

def rotary_tables(length, width):
    half = width // 2
    position = jnp.arange(length, dtype=jnp.float32)
    inverse = THETA ** (-(jnp.arange(half, dtype=jnp.float32) * 2.0) / width)
    angles = position[:, None] * inverse[None, :]
    return (jnp.cos(angles)[:, None, :], jnp.sin(angles)[:, None, :])

def rotate(values, cosine, sine):
    half = values.shape[-1] // 2
    first = values[..., :half]
    second = values[..., half:]
    return jnp.concatenate([first * cosine - second * sine, second * cosine + first * sine], axis=-1)

def attend(query_block, keys, values, start):
    block = query_block.shape[1]
    length = keys.shape[1]
    scores = jnp.einsum('gqkrd,gtkd->gkrqt', query_block, keys, precision=HIGH) * HEAD_DIM ** (-0.5)
    scores = low_back(scores)
    allowed = jnp.arange(length)[None, :] <= (start + jnp.arange(block))[:, None]
    scores = jnp.where(allowed, scores, -1e+30)
    peak = lax.optimization_barrier(jnp.max(scores, axis=-1, keepdims=True))
    expo = jnp.exp(scores - peak)
    probs = low(expo / lax.optimization_barrier(jnp.sum(expo, axis=-1, keepdims=True)))
    return jnp.einsum('gkrqt,gtkd->gqkrd', probs, values, precision=HIGH)

def layer(inputs, gain_one, query_weight, key_weight, value_weight, out_weight, gain_two, gate_weight, up_weight, down_weight):
    groups, length, width = inputs.shape
    per_group = HEADS // KV_HEADS
    cosine, sine = rotary_tables(length, HEAD_DIM)
    inv_one = lax.rsqrt(lax.optimization_barrier(jnp.mean(inputs * inputs, axis=-1, keepdims=True)) + EPSILON)
    normed_one = low(inputs * inv_one * gain_one)
    query_raw = low_back(jnp.einsum('gsd,de->gse', normed_one, query_weight, precision=HIGH))
    key_raw = low_back(jnp.einsum('gsd,de->gse', normed_one, key_weight, precision=HIGH))
    value_raw = jnp.einsum('gsd,de->gse', normed_one, value_weight, precision=HIGH)
    query_rot = low(rotate(query_raw.reshape(groups, length, HEADS, HEAD_DIM), cosine, sine))
    key_rot = low(rotate(key_raw.reshape(groups, length, KV_HEADS, HEAD_DIM), cosine, sine))
    value_low = low(low_back(value_raw)).reshape(groups, length, KV_HEADS, HEAD_DIM)
    query_rot = query_rot.reshape(groups, length, KV_HEADS, per_group, HEAD_DIM)
    qblock = 512 if length % 512 == 0 else length
    pieces = []
    for index in range(length // qblock):
        start = index * qblock
        step_fn = jax.checkpoint(partial(attend, start=start))
        pieces.append(step_fn(query_rot[:, start:start + qblock], key_rot, value_low))
    attended = jnp.concatenate(pieces, axis=1).reshape(groups, length, HEADS * HEAD_DIM)
    attended = low(low_back(attended))
    mixed = inputs + low_back(jnp.einsum('gse,ed->gsd', attended, out_weight, precision=HIGH))
    inv_two = lax.rsqrt(lax.optimization_barrier(jnp.mean(mixed * mixed, axis=-1, keepdims=True)) + EPSILON)
    normed_two = low(mixed * inv_two * gain_two)
    gate_val = low_back(jnp.einsum('gsd,df->gsf', normed_two, gate_weight, precision=HIGH))
    up_val = low_back(jnp.einsum('gsd,df->gsf', normed_two, up_weight, precision=HIGH))
    hidden = low(jax.nn.silu(gate_val) * up_val)
    branch = low_back(jnp.einsum('gsf,fd->gsd', hidden, down_weight, precision=HIGH))
    return mixed + branch

def reference(tokens, norm1_gain, w_query, w_key, w_value, w_out, norm2_gain, w_gate, w_up, w_down, cotangent):
    length = SEQ
    count = tokens.shape[0] // length
    group = math.gcd(count, max(1, 4096 // length))
    steps_total = count // group
    params = tuple((w.astype(jnp.float32) for w in (norm1_gain, w_query, w_key, w_value, w_out, norm2_gain, w_gate, w_up, w_down)))
    inputs = tokens.astype(jnp.float32).reshape(steps_total, group, length, D)
    cots = cotangent.astype(jnp.float32).reshape(steps_total, group, length, D)
    zeros = tuple((jnp.zeros(w.shape, jnp.float32) for w in params))

    def one_step(carry, item):
        batch, cot = item
        result, pullback = jax.vjp(layer, batch, *params)
        grads = pullback(cot)
        carry = tuple((c + g for c, g in zip(carry, grads[1:])))
        return (carry, (result.astype(jnp.bfloat16), grads[0]))
    totals, (results, input_grads) = lax.scan(one_step, zeros, (inputs, cots))
    output = results.reshape(count * length, D)
    grad_tokens = input_grads.reshape(count * length, D)
    return (output, grad_tokens, totals[0], totals[1], totals[2], totals[3], totals[4], totals[5], totals[6], totals[7], totals[8])
```

```python
import functools
import types

import jax
import jax.numpy as jnp
from jax import lax
from jax.experimental import pallas as pl
from jax.experimental.pallas import tpu as pltpu
from jax.sharding import PartitionSpec as P

HEADS = 16
KV_HEADS = 8
HEAD_DIM = 96
EPSILON = 1e-05
THETA = 100000.0

AXIS = "fsdp"
GROUP = 8
MESH = pl.DeviceIdType.MESH
BF = jnp.bfloat16
F32 = jnp.float32
ANY = pl.BlockSpec(memory_space=pl.ANY)
VM = pl.BlockSpec(memory_space=pltpu.VMEM)
DMA = pltpu.SemaphoreType.DMA


def place():
    me = lax.axis_index(AXIS)
    p, r = lax.rem(me, GROUP), lax.div(me, GROUP)
    c = lax.rem(me, 2)
    x = lax.rem(lax.div(me, 2), 2)
    y = lax.rem(lax.div(me, 4), 2)
    to_x, to_y, to_c = 2 - 4 * x, 4 - 8 * y, 1 - 2 * c
    k0 = y * 2 + x
    kx, ky = k0 + 1 - 2 * x, k0 + 2 - 4 * y
    return types.SimpleNamespace(
        me=me, p=p, r=r, c=c, core=me + to_c, xn=me + to_x, yn=me + to_y,
        up=me + GROUP, dn=me - GROUP, to_c=to_c,
        px=p + to_x, py=p + to_y, pd=p + to_x + to_y,
        k0=k0, kx=kx, ky=ky, kd=kx + ky - k0,
    )


def when(cond, do):
    if cond is None:
        do()
    else:
        pl.when(cond)(do)


def both(a, b):
    if a is None:
        return b
    if b is None:
        return a
    return jnp.logical_and(a, b)


class Book:
    def __init__(self, at):
        self.at, self.sent = at, []

    def send(self, src, dst, ss, rs, dev, cond=None):
        def copy():
            return pltpu.make_async_remote_copy(
                src_ref=src, dst_ref=dst, send_sem=ss, recv_sem=rs,
                device_id=(dev,), device_id_type=MESH,
            )

        when(cond, lambda: copy().start())
        self.sent.append((cond, copy))

    def got(self, dst, rs, cond=None):
        def wait():
            pltpu.make_async_remote_copy(
                src_ref=dst, dst_ref=dst, send_sem=rs, recv_sem=rs,
                device_id=(self.at.core,), device_id_type=MESH,
            ).wait_recv()

        when(cond, wait)

    def drain(self):
        for cond, copy in self.sent:
            when(cond, lambda: copy().wait_send())


def meet(at, groups, plane, line):
    bar = pltpu.get_barrier_semaphore()

    def greet(dev):
        pl.semaphore_signal(bar, inc=1, device_id=(dev,), device_id_type=MESH)

    if plane == "all":
        peers = [at.me - at.p + lax.rem(at.p + k, GROUP) for k in range(1, GROUP)]
    else:
        peers = [at.core, at.xn, at.yn]
    for dev in peers:
        greet(dev)
    count = len(peers)
    if line:
        pl.when(at.r < groups - 1)(lambda: greet(at.up))
        pl.when(at.r > 0)(lambda: greet(at.dn))
        ends = jnp.where(at.r > 0, 1, 0) + jnp.where(at.r < groups - 1, 1, 0)
        count = count + ends
    pl.semaphore_wait(bar, count)


class PlaneGather:
    def __init__(self, at, book, pos, rs, ss):
        self.at, self.book, self.pos, self.rs, self.ss = at, book, pos, rs, ss

    def own(self, i, src, cond=None):
        at, dst, rs = self.at, self.pos(i, self.at.p), self.rs(i, self.at.p)
        self.book.send(src, dst, self.ss(i, 0), rs, at.xn, cond)
        self.book.send(src, dst, self.ss(i, 1), rs, at.yn, cond)
        self.book.send(src, dst, self.ss(i, 2), rs, at.core, cond)

    def event(self, i, odd, cond=None):
        at = self.at
        for q, kind in ((at.px, 3), (at.py, 5), (at.pd, 7)):
            dst, rs = self.pos(i, q), self.rs(i, q)
            self.book.got(dst, rs, cond)
            if kind == 3:
                self.fwd(dst, self.ss(i, 4), rs, at.yn, cond, odd, True)
            if kind == 5:
                self.fwd(dst, self.ss(i, 6), rs, at.xn, cond, odd, False)
            self.book.send(dst, dst, self.ss(i, kind), rs, at.core, cond)

    def fwd(self, dst, ss, rs, dev, cond, odd, on_odd):
        if isinstance(odd, bool):
            if odd == on_odd:
                self.book.send(dst, dst, ss, rs, dev, cond)
        else:
            mine = odd if on_odd else jnp.logical_not(odd)
            self.book.send(dst, dst, ss, rs, dev, both(cond, mine))

    def finish(self, i, cond=None):
        at = self.at
        for q in (at.p, at.px, at.py, at.pd):
            q = q + at.to_c
            self.book.got(self.pos(i, q), self.rs(i, q), cond)


class LineGather:
    def __init__(self, at, book, groups, pos, rs, ss):
        self.at, self.book, self.groups = at, book, groups
        self.pos, self.rs, self.ss = pos, rs, ss

    def own(self, src):
        r, dst = self.at.r, self.pos(self.at.r)
        self.book.send(src, dst, self.ss(r, 0), self.rs(r), self.at.up, r < self.groups - 1)
        self.book.send(src, dst, self.ss(r, 1), self.rs(r), self.at.dn, r > 0)

    def step(self, d, then=None):
        r, last = self.at.r, self.groups - 1
        below, above = r >= d, r + d <= last
        for q, here, go, kind, dev in (
            (r - d, below, r < last, 0, self.at.up),
            (r + d, above, r > 0, 1, self.at.dn),
        ):
            dst = self.pos(q)
            self.book.got(dst, self.rs(q), here)
            self.book.send(dst, dst, self.ss(q, kind), self.rs(q), dev, both(here, go))
            if then is not None:
                then(q, here, dst)


def around(r, d, last):
    if d == 0:
        return [(r, None)]
    return [(r - d, r >= d), (r + d, r + d <= last)]


def gather_kernel(
    R, NE, q_i, o_i, gu_i, wd_i, e_i, q_o, o_o, gu_o, wd_o, e_o,
    lsem, qr, qz, qp, orr, oz, op, gar, gas, gzr, gzs, dr, ds_, er, es,
):
    at = place()
    meet(at, R, "all", True)
    book = Book(at)
    r, last = at.r, R - 1

    def full(inp, out, rs, zs, ps):
        def slot(i, q):
            return i * GROUP + q

        plane = PlaneGather(
            at, book, lambda i, q: out.at[slot(i, q)], lambda i, q: rs.at[slot(i, q)],
            lambda i, k: ps.at[i, k],
        )
        line = LineGather(
            at, book, R, lambda i: out.at[slot(i, at.p)], lambda i: rs.at[slot(i, at.p)],
            lambda i, k: zs.at[i, k],
        )

        def events(d):
            for i, cond in around(r, d, last):
                plane.event(i, lax.rem(i, 2) == 1, cond)

        def finish(d):
            for i, cond in around(r, d, last):
                plane.finish(i, cond)

        return types.SimpleNamespace(
            start=lambda: (line.own(inp), plane.own(r, inp)),
            line=lambda d: line.step(d, lambda i, cond, dst: plane.own(i, dst, cond)),
            events=events, finish=finish,
        )

    q = full(q_i, q_o, qr, qz, qp)
    o = full(o_i, o_o, orr, oz, op)
    q.start()
    o.start()
    mine = [
        pltpu.make_async_copy(q_i, q_o.at[at.me], lsem.at[0]),
        pltpu.make_async_copy(o_i, o_o.at[at.me], lsem.at[1]),
        pltpu.make_async_copy(gu_i.at[at.p], gu_o.at[at.me], lsem.at[2]),
        pltpu.make_async_copy(wd_i, wd_o.at[r], lsem.at[3]),
        pltpu.make_async_copy(e_i, e_o.at[at.p], lsem.at[4]),
    ]
    for copy in mine:
        copy.start()
    for k in range(1, GROUP):
        t = lax.rem(at.p + k, GROUP)
        book.send(gu_i.at[t], gu_o.at[at.me], gas.at[k - 1], gar.at[k - 1], at.me - at.p + t)

    gu_line = LineGather(
        at, book, R, lambda i: gu_o.at[pl.ds(i * GROUP, GROUP)], lambda i: gzr.at[i],
        lambda i, k: gzs.at[i, k],
    )
    wd_line = LineGather(
        at, book, R, lambda i: wd_o.at[i], lambda i: dr.at[i], lambda i, k: ds_.at[i, k]
    )

    for d in range(1, R):
        q.line(d)
        o.line(d)
        q.events(d - 1)
        if d == max(1, R - 2):
            for k in range(1, GROUP):
                t = lax.rem(at.p + GROUP - k, GROUP)
                book.got(gu_o.at[r * GROUP + t], gar.at[k - 1])
            for copy in mine:
                copy.wait()
    gu_line.own(gu_o.at[pl.ds(r * GROUP, GROUP)])
    wd_line.own(wd_i)
    q.events(R - 1)
    o.events(0)
    for d in range(1, R):
        if d == 2:
            e_events = e_start(at, book, NE, e_i, e_o, er, es)
        gu_line.step(d)
        o.events(d)
        wd_line.step(d)
        if d == R - 2:
            e_events()
    for d in range(R):
        q.finish(d)
        o.finish(d)
    e_events(True)
    book.drain()


def e_start(at, book, parts, e_i, e_o, er, es):
    rows = e_i.shape[0] // parts

    def part(i):
        return pl.ds(i * rows, rows)

    plane = PlaneGather(
        at, book, lambda i, q: e_o.at[q, part(i)], lambda i, q: er.at[i, q],
        lambda i, k: es.at[i, k],
    )
    for i in range(parts):
        plane.own(i, e_i.at[part(i)])

    def events(finish=False):
        for i in range(parts):
            if finish:
                plane.finish(i)
            else:
                plane.event(i, i % 2 == 1)

    return events


def gather_weights(R, q, o, gu, wd, e):
    n = R * GROUP
    rows, parts = q.shape[0], 4
    return pl.pallas_call(
        functools.partial(gather_kernel, R, parts),
        out_shape=(
            jax.ShapeDtypeStruct((n, rows, q.shape[1]), BF),
            jax.ShapeDtypeStruct((n, rows, o.shape[1]), BF),
            jax.ShapeDtypeStruct((n, rows, gu.shape[2]), BF),
            jax.ShapeDtypeStruct((R,) + wd.shape, BF),
            jax.ShapeDtypeStruct((GROUP,) + e.shape, BF),
        ),
        in_specs=[ANY] * 5,
        out_specs=(ANY,) * 5,
        scratch_shapes=[
            DMA((5,)),
            DMA((n,)), DMA((R, 2)), DMA((R, 8)),
            DMA((n,)), DMA((R, 2)), DMA((R, 8)),
            DMA((7,)), DMA((7,)), DMA((R,)), DMA((R, 2)),
            DMA((R,)), DMA((R, 2)),
            DMA((parts, GROUP)), DMA((parts, 8)),
        ],
        compiler_params=pltpu.CompilerParams(collective_id=0, has_side_effects=True),
    )(q, o, gu, wd, e)


def spread_kernel(parts, a_i, a_o, lsem, er, es):
    at = place()
    meet(at, 1, "near", False)
    book = Book(at)
    own = pltpu.make_async_copy(a_i, a_o.at[at.p], lsem)
    own.start()
    events = e_start(at, book, parts, a_i, a_o, er, es)
    events()
    events(True)
    own.wait()
    book.drain()


def spread(a):
    parts = 4
    return pl.pallas_call(
        functools.partial(spread_kernel, parts),
        out_shape=jax.ShapeDtypeStruct((GROUP,) + a.shape, a.dtype),
        in_specs=[ANY],
        out_specs=ANY,
        scratch_shapes=[DMA, DMA((parts, GROUP)), DMA((parts, 8))],
        compiler_params=pltpu.CompilerParams(collective_id=1, has_side_effects=True),
    )(a)


def add_rows(out, terms):
    step = 16

    def body(i, carry):
        at = pl.ds(pl.multiple_of(i * step, step), step)
        total = terms[0][at, :].astype(F32)
        for term in terms[1:]:
            total = total + term[at, :].astype(F32)
        out[at, :] = total.astype(out.dtype)
        return carry

    lax.fori_loop(0, out.shape[0] // step, body, 0)


class PlaneSum:
    def __init__(self, at, book, odd, pairs, mine, other, diag, from_x, from_y, sem):
        self.at, self.book, self.odd, self.pairs = at, book, odd, pairs
        self.mine, self.other, self.diag = mine, other, diag
        self.from_x, self.from_y, self.sem = from_x, from_y, sem

    def loads(self):
        c = self.at.c
        return [
            pltpu.make_async_copy(src(c), dst(self.mine), self.sem(j))
            for j, (src, dst) in enumerate(self.pairs)
        ]

    def start(self):
        for load in self.loads():
            load.start()
        for j, (src, dst) in enumerate(self.pairs):
            self.book.send(
                src(1 - self.at.c), dst(self.other), self.sem(2 + j), self.sem(4 + j), self.at.core
            )

    def fold(self, k):
        add_rows(self.mine.at[k], [self.mine.at[k], self.other.at[k]])

    def first(self):
        at, book = self.at, self.book
        for load in self.loads():
            load.wait()
        for j, (src, dst) in enumerate(self.pairs):
            book.got(dst(self.other), self.sem(4 + j))
        dev = at.yn if self.odd else at.xn
        self.fold(at.kd)
        book.send(self.mine.at[at.kd], self.diag, self.sem(6), self.sem(7), dev)
        if self.odd:
            self.fold(at.ky)
            book.send(self.mine.at[at.ky], self.from_y, self.sem(8), self.sem(9), at.yn)
            self.fold(at.kx)
        else:
            self.fold(at.kx)
            book.send(self.mine.at[at.kx], self.from_x, self.sem(8), self.sem(9), at.xn)
            self.fold(at.ky)
        self.fold(at.k0)

    def second(self):
        at, book = self.at, self.book
        book.got(self.diag, self.sem(7))
        k = at.kx if self.odd else at.ky
        add_rows(self.mine.at[k], [self.mine.at[k], self.diag])
        if self.odd:
            book.send(self.mine.at[at.kx], self.from_x, self.sem(10), self.sem(11), at.xn)
        else:
            book.send(self.mine.at[at.ky], self.from_y, self.sem(10), self.sem(11), at.yn)

    def third(self, out):
        at, book = self.at, self.book
        book.got(self.from_x, self.sem(11 if self.odd else 9))
        book.got(self.from_y, self.sem(9 if self.odd else 11))
        add_rows(out, [self.mine.at[at.k0], self.from_x, self.from_y])


def row_items(at, book, src, parts, mine, other, diag, from_x, from_y, sems):
    rows = src.shape[2] // parts
    items = []
    for i in range(parts):
        cut = pl.ds(i * rows, rows)
        items.append(
            PlaneSum(
                at, book, i % 2 == 1,
                [(lambda c, cut=cut: src.at[:, c, cut], lambda buf: buf)],
                mine.at[i], other.at[i], diag.at[i], from_x.at[i], from_y.at[i],
                lambda j, i=i: sems.at[i, j],
            )
        )
    return items


def row_scratch(parts, rows, columns):
    rows = rows // parts
    return [
        pltpu.VMEM((parts, 4, rows, columns), BF),
        pltpu.VMEM((parts, 4, rows, columns), BF),
        pltpu.VMEM((parts, rows, columns), BF),
        pltpu.VMEM((parts, rows, columns), BF),
        pltpu.VMEM((parts, rows, columns), BF),
        DMA((parts, 12)),
    ]


def fold_kernel(parts, a_i, a_o, mine, other, diag, from_x, from_y, sems):
    at = place()
    meet(at, 1, "near", False)
    book = Book(at)
    items = row_items(at, book, a_i, parts, mine, other, diag, from_x, from_y, sems)
    rows = a_o.shape[0] // parts
    for item in items:
        item.start()
    for i in range(parts + 2):
        if i < parts:
            items[i].first()
        if 1 <= i <= parts:
            items[i - 1].second()
        if i >= 2:
            items[i - 2].third(a_o.at[pl.ds((i - 2) * rows, rows)])
    book.drain()


def fold(a):
    parts = 4
    rows, columns = a.shape[2:]
    return pl.pallas_call(
        functools.partial(fold_kernel, parts),
        out_shape=jax.ShapeDtypeStruct((rows, columns), F32),
        in_specs=[ANY],
        out_specs=VM,
        scratch_shapes=row_scratch(parts, rows, columns),
        compiler_params=pltpu.CompilerParams(
            collective_id=2, has_side_effects=True, vmem_limit_bytes=50 * 2**20
        ),
    )(a)


class LineSum:
    def __init__(self, at, book, groups, whole, part, inbox, views, rs, ss):
        self.at, self.book, self.groups, self.whole = at, book, groups, whole
        self.part, self.inbox, self.views, self.rs, self.ss = part, inbox, views, rs, ss

    def add(self, i, cond):
        def do():
            self.book.got(self.inbox(i), self.rs(i))
            for a, b in zip(self.views(self.part(i)), self.views(self.inbox(i))):
                add_rows(a, [a, b])

        pl.when(cond)(do)

    def step(self, t):
        r, last = self.at.r, self.groups - 1
        i = last - t + r
        go = jnp.logical_and(t >= r, r < last)
        self.add(i, jnp.logical_and(go, r > 0))
        self.book.send(self.part(i), self.inbox(i), self.ss(0, t), self.rs(i), self.at.up, go)
        m = last - r
        i = t - m
        go = jnp.logical_and(t >= m, r > 0)
        self.add(i, jnp.logical_and(go, r < last))
        to = jnp.where(i == r - 1, self.groups, i)
        self.book.send(self.part(i), self.inbox(to), self.ss(1, t), self.rs(to), self.at.dn, go)

    def final(self, outs):
        r, last = self.at.r, self.groups - 1
        up, dn = self.inbox(r), self.inbox(self.groups)

        def total(refs):
            for out, *terms in zip(outs, *[self.views(ref) for ref in refs]):
                add_rows(out, terms)

        self.book.got(up, self.rs(r), r > 0)
        self.book.got(dn, self.rs(self.groups), r < last)
        mine = self.part(r)
        pl.when(r == 0)(lambda: total([mine, dn]))
        pl.when(r == last)(lambda: total([mine, up]))
        pl.when(jnp.logical_and(r > 0, r < last))(lambda: total([mine, up, dn]))


def sum_kernel(
    R, parts, q_i, gc_i, o_i, gu_i, wd_i, y_i, q_o, o_o, gu_o, wd_o, y_o,
    qm, qc, qd, qx, qy, qs, om, oc, od, ox, oy, os_, qz, qzr, qzs, oz, ozr, ozs,
    gm, gz, gzr, gzs, dm, dz, dzr, dzs, gf, gas, gar, lsem,
    ym, yc, yd, yx, yy, ys,
):
    at = place()
    meet(at, R, "all", True)
    book = Book(at)
    r = at.r
    wide = q_i.shape[-1]

    def whole(ref):
        return [ref]

    def many(ref):
        return [ref.at[j] for j in range(GROUP)]

    gm_load = pltpu.make_async_copy(gu_i, gm, lsem.at[0])
    dm_load = pltpu.make_async_copy(wd_i, dm, lsem.at[1])
    gm_load.start()
    dm_load.start()

    order = []
    for i in range((R + 1) // 2):
        order += [R - 1 - i] + ([i] if i < R - 1 - i else [])
    items, outs = [], []
    for i in order:
        items.append(
            PlaneSum(
                at, book, i % 2 == 1, [(lambda c, i=i: o_i.at[i, :, c], lambda buf: buf)],
                om.at[i], oc.at[i], od.at[i], ox.at[i], oy.at[i], lambda j, i=i: os_.at[i, j],
            )
        )
        outs.append(om.at[i, at.k0])
    for i in order:
        items.append(
            PlaneSum(
                at, book, i % 2 == 1,
                [
                    (lambda c, i=i: q_i.at[i, :, c], lambda buf: buf.at[:, :, pl.ds(0, wide)]),
                    (lambda c, i=i: gc_i.at[i, :, c], lambda buf: buf.at[:, :, pl.ds(wide, 128)]),
                ],
                qm.at[i], qc.at[i], qd.at[i], qx.at[i], qy.at[i], lambda j, i=i: qs.at[i, j],
            )
        )
        outs.append(qm.at[i, at.k0])
    attn = len(items)
    items += row_items(at, book, y_i, parts, ym, yc, yd, yx, yy, ys)
    rows = y_o.shape[0] // parts
    outs += [y_o.at[pl.ds(i * rows, rows)] for i in range(parts)]

    gu_sum = LineSum(
        at, book, R, None, lambda i: gm.at[i], lambda i: gz.at[i], many,
        lambda i: gzr.at[i], lambda k, t: gzs.at[k, t],
    )
    wd_sum = LineSum(
        at, book, R, None, lambda i: dm.at[i], lambda i: dz.at[i], whole,
        lambda i: dzr.at[i], lambda k, t: dzs.at[k, t],
    )
    q_sum = LineSum(
        at, book, R, None, lambda i: qm.at[i, at.k0], lambda i: qz.at[i], whole,
        lambda i: qzr.at[i], lambda k, t: qzs.at[k, t],
    )
    o_sum = LineSum(
        at, book, R, None, lambda i: om.at[i, at.k0], lambda i: oz.at[i], whole,
        lambda i: ozr.at[i], lambda k, t: ozs.at[k, t],
    )

    for item in items[:attn]:
        item.start()
    dm_load.wait()
    gm_load.wait()

    own = pltpu.make_async_copy(gf.at[at.p], gu_o.at[at.p], lsem.at[2])

    def mlp_end():
        gu_sum.final(many(gf))
        own.start()
        for k in range(1, GROUP):
            t = lax.rem(at.p + k, GROUP)
            book.send(gf.at[t], gu_o.at[at.p], gas.at[k - 1], gar.at[k - 1], at.me - at.p + t)
        wd_sum.final(whole(wd_o))

    def mlp(t):
        gu_sum.step(t)
        wd_sum.step(t)

    def att(t):
        o_sum.step(t)
        q_sum.step(t)

    hooks = {}
    for t in range(R - 1):
        hooks.setdefault((t * attn) // (R - 1), []).append(functools.partial(mlp, t))
        hooks.setdefault(attn + 2 + (t * parts) // (R - 1), []).append(functools.partial(att, t))
    hooks.setdefault(attn + 2, []).append(mlp_end)

    total = len(items)
    for i in range(total + 2):
        for hook in hooks.get(i, ()):
            hook()
        if i == 2:
            for item in items[attn:]:
                item.start()
        if i < total:
            items[i].first()
        if 1 <= i <= total:
            items[i - 1].second()
        if i >= 2:
            items[i - 2].third(outs[i - 2])
    q_sum.final(whole(q_o))
    o_sum.final(whole(o_o))
    for k in range(1, GROUP):
        t = lax.rem(at.p + GROUP - k, GROUP)
        book.got(gu_o.at[t], gar.at[k - 1])
    own.wait()
    book.drain()


def sum_all(R, q, gc, o, gu, wd, y):
    rows, parts = q.shape[3], 4
    wide, mid, two = q.shape[4] + gc.shape[4], o.shape[4], gu.shape[3]
    deep, width = wd.shape[1:]
    steps = max(R - 1, 1)

    def attn(columns):
        return [
            pltpu.VMEM((R, 4, rows, columns), BF),
            pltpu.VMEM((R, 4, rows, columns), BF),
            pltpu.VMEM((R, rows, columns), BF),
            pltpu.VMEM((R, rows, columns), BF),
            pltpu.VMEM((R, rows, columns), BF),
            DMA((R, 12)),
        ]

    return pl.pallas_call(
        functools.partial(sum_kernel, R, parts),
        out_shape=(
            jax.ShapeDtypeStruct((rows, wide), F32),
            jax.ShapeDtypeStruct((rows, mid), F32),
            jax.ShapeDtypeStruct((GROUP, rows, two), BF),
            jax.ShapeDtypeStruct((deep, width), F32),
            jax.ShapeDtypeStruct(y.shape[2:], F32),
        ),
        in_specs=[ANY] * 6,
        out_specs=(VM, VM, ANY, VM, VM),
        scratch_shapes=attn(wide) + attn(mid) + [
            pltpu.VMEM((R + 1, rows, wide), BF), DMA((R + 1,)), DMA((2, steps)),
            pltpu.VMEM((R + 1, rows, mid), BF), DMA((R + 1,)), DMA((2, steps)),
            pltpu.VMEM((R, GROUP, rows, two), BF), pltpu.VMEM((R + 1, GROUP, rows, two), BF),
            DMA((R + 1,)), DMA((2, steps)),
            pltpu.VMEM((R, deep, width), BF), pltpu.VMEM((R + 1, deep, width), BF),
            DMA((R + 1,)), DMA((2, steps)),
            pltpu.VMEM((GROUP, rows, two), BF), DMA((7,)), DMA((7,)), DMA((3,)),
        ] + row_scratch(parts, *y.shape[2:]),
        compiler_params=pltpu.CompilerParams(
            collective_id=3, has_side_effects=True, vmem_limit_bytes=60 * 2**20
        ),
    )(q, gc, o, gu, wd, y)


def rotary_tables(length, width):
    half = width // 2
    position = jnp.arange(length, dtype=jnp.float32)
    inverse = THETA ** (-(jnp.arange(half, dtype=jnp.float32) * 2.0) / width)
    angles = position[:, None] * inverse[None, :]
    return (jnp.cos(angles)[:, None, :], jnp.sin(angles)[:, None, :])


def rotate(values, cosine, sine):
    half = values.shape[-1] // 2
    first = values[..., :half]
    second = values[..., half:]
    return jnp.concatenate(
        [first * cosine - second * sine, second * cosine + first * sine], axis=-1
    )


def rotate_back(grads, cosine, sine):
    half = grads.shape[-1] // 2
    first = grads[..., :half]
    second = grads[..., half:]
    return jnp.concatenate(
        [first * cosine + second * sine, second * cosine - first * sine], axis=-1
    )


def matmul(left, right):
    return jnp.dot(left, right, preferred_element_type=jnp.float32)


def rows_inner(left, right):
    return lax.dot_general(
        left, right, (((0,), (0,)), ((), ())), preferred_element_type=jnp.float32
    )


def times_transposed(left, right):
    return lax.dot_general(
        left, right, (((1,), (1,)), ((), ())), preferred_element_type=jnp.float32
    )


def rms_forward(values, gain):
    inverse = lax.rsqrt(jnp.mean(values * values, axis=-1, keepdims=True) + EPSILON)
    normed = values * inverse
    return (normed, inverse, (normed * gain).astype(jnp.bfloat16))


def rms_backward(grad_in, normed, inverse, gain):
    scaled = grad_in * gain
    gain_grad = jnp.sum(grad_in * normed, axis=0)
    input_grad = inverse * (scaled - normed * jnp.mean(scaled * normed, axis=-1, keepdims=True))
    return (input_grad, gain_grad)


def block_scores(query_rot, key_rot, scale):
    length = query_rot.shape[0]
    scores = (
        jnp.einsum("qkrd,tkd->krqt", query_rot, key_rot, preferred_element_type=jnp.float32) * scale
    )
    allowed = jnp.arange(length)[None, :] <= jnp.arange(length)[:, None]
    return jnp.where(allowed, scores, -1e30)


def pad_rows(array, axis, rows):
    pad = [(0, 0)] * array.ndim
    pad[axis] = (0, rows - array.shape[axis])
    return jnp.pad(array, pad) if rows != array.shape[axis] else array


def body(
    R, tokens, norm1_gain, w_query, w_key, w_value, w_out, norm2_gain, w_gate, w_up, w_down, cotangent
):
    length, width = tokens.shape
    n = R * GROUP
    own = w_query.shape[0]
    rows = -(-own // 16) * 16
    deep = w_down.shape[0]
    per_group = HEADS // KV_HEADS
    scale = HEAD_DIM ** (-0.5)
    cosine, sine = rotary_tables(length, HEAD_DIM)
    nq, nk = HEADS * HEAD_DIM, KV_HEADS * HEAD_DIM

    gains = jnp.concatenate([norm1_gain[:, None], norm2_gain[:, None]], axis=1)
    q_shard = pad_rows(
        jnp.concatenate([w_query, w_key, w_value, jnp.pad(gains, ((0, 0), (0, 126)))], axis=1), 0, rows
    )
    o_shard = pad_rows(w_out, 0, rows)

    def by_place(w):
        return w.reshape(own, R, GROUP, deep).transpose(2, 0, 1, 3).reshape(GROUP, own, R * deep)

    gu_shard = pad_rows(jnp.concatenate([by_place(w_gate), by_place(w_up)], axis=2), 1, rows)
    q_all, o_all, gu_all, wd_all, e_all = gather_weights(
        R, q_shard, o_shard, gu_shard, w_down, cotangent
    )

    def whole(a):
        return a[:, :own].reshape(n * own, a.shape[2])

    qkv_weight, out_weight, gu_weight = whole(q_all), whole(o_all), whole(gu_all)
    down_weight = wd_all.reshape(R * deep, width)
    gain_one = qkv_weight[:, nq + 2 * nk].astype(F32)
    gain_two = qkv_weight[:, nq + 2 * nk + 1].astype(F32)

    inputs = tokens.astype(jnp.float32)
    normed_one, inv_one, act_one = rms_forward(inputs, gain_one)
    raw = matmul(act_one, qkv_weight)
    query_raw = raw[:, :nq].reshape(length, HEADS, HEAD_DIM)
    key_raw = raw[:, nq : nq + nk].reshape(length, KV_HEADS, HEAD_DIM)
    value_low = raw[:, nq + nk : nq + 2 * nk].astype(BF).reshape(length, KV_HEADS, HEAD_DIM)
    query_rot = (
        rotate(query_raw, cosine, sine).astype(BF).reshape(length, KV_HEADS, per_group, HEAD_DIM)
    )
    key_rot = rotate(key_raw, cosine, sine).astype(BF)
    scores = block_scores(query_rot, key_rot, scale)
    peak = jnp.max(scores, axis=-1, keepdims=True)
    expo = jnp.exp(scores - peak)
    total = jnp.sum(expo, axis=-1, keepdims=True)
    probs = (expo / total).astype(BF)
    lse = peak + jnp.log(total)
    heads_out = jnp.einsum("krqt,tkd->qkrd", probs, value_low, preferred_element_type=F32)
    attended = heads_out.reshape(length, nq).astype(BF)
    mixed = inputs + matmul(attended, out_weight)
    normed_two, inv_two, act_two = rms_forward(mixed, gain_two)

    act_all = spread(act_two).reshape(GROUP * length, width)
    cot_all = e_all.reshape(GROUP * length, width)
    hid = R * deep
    pair = matmul(act_all, gu_weight)
    gate_val, up_val = pair[:, :hid], pair[:, hid:]
    sigma = jax.nn.sigmoid(gate_val)
    silu_val = gate_val * sigma
    hidden = (silu_val * up_val).astype(BF)
    out_part = matmul(hidden, down_weight).astype(BF)
    hidden_grad = times_transposed(cot_all, down_weight)
    gate_grad_b = (hidden_grad * up_val * sigma * (1.0 + gate_val * (1.0 - sigma))).astype(BF)
    up_grad_b = (hidden_grad * silu_val).astype(BF)
    pair_grad = jnp.concatenate([gate_grad_b, up_grad_b], axis=1)
    act_part = times_transposed(pair_grad, gu_weight).astype(BF)
    act_two_grad = fold(act_part.reshape(4, 2, length, width))
    gu_part = rows_inner(act_all, pair_grad).astype(BF)
    wd_part = rows_inner(hidden, cot_all).astype(BF)

    grad_out = cotangent.astype(jnp.float32)
    mixed_part, gain_two_grad = rms_backward(act_two_grad, normed_two, inv_two, gain_two)
    mixed_grad = grad_out + mixed_part

    branch_grad = mixed_grad.astype(BF)
    attended_grad = (
        times_transposed(branch_grad, out_weight)
        .astype(BF)
        .reshape(length, KV_HEADS, per_group, HEAD_DIM)
    )
    scores = block_scores(query_rot, key_rot, scale)
    probs = jnp.exp(scores - lse)
    probs_low = probs.astype(BF)
    prob_grad = jnp.einsum(
        "qkrd,tkd->krqt", attended_grad, value_low, preferred_element_type=jnp.float32
    )
    center = jnp.sum(probs * prob_grad, axis=-1, keepdims=True)
    score_grad = (probs * (prob_grad - center)).astype(BF)
    query_grads = (
        jnp.einsum("krqt,tkd->qkrd", score_grad, key_rot, preferred_element_type=jnp.float32)
        * scale
    )
    key_term = (
        jnp.einsum("krqt,qkrd->tkd", score_grad, query_rot, preferred_element_type=jnp.float32)
        * scale
    )
    value_term = jnp.einsum(
        "krqt,qkrd->tkd", probs_low, attended_grad, preferred_element_type=jnp.float32
    )
    query_raw_grad = (
        rotate_back(query_grads.reshape(length, HEADS, HEAD_DIM), cosine, sine)
        .astype(BF)
        .reshape(length, nq)
    )
    key_raw_grad = rotate_back(key_term, cosine, sine).astype(BF).reshape(length, nk)
    value_raw_grad = value_term.astype(BF).reshape(length, nk)
    raw_grad = jnp.concatenate([query_raw_grad, key_raw_grad, value_raw_grad], axis=1)
    qkv_part = rows_inner(act_one, raw_grad).astype(BF)
    raw_grad_wide = jnp.pad(raw_grad, ((0, 0), (0, 128)))
    act_one_grad = times_transposed(raw_grad_wide, qkv_weight)
    input_part, gain_one_grad = rms_backward(act_one_grad, normed_one, inv_one, gain_one)
    grad_tokens = mixed_grad + input_part
    o_part = rows_inner(attended, branch_grad).astype(BF)
    gain_part = jnp.pad(
        jnp.stack([gain_one_grad, gain_two_grad], axis=1), ((0, 0), (0, 126))
    ).astype(BF)

    def split(a):
        return pad_rows(a.reshape(R, 4, 2, own, a.shape[1]), 3, rows)

    q_sum, o_sum, gu_sum, wd_sum, out_sum = sum_all(
        R,
        split(qkv_part),
        split(gain_part),
        split(o_part),
        pad_rows(gu_part.reshape(R, GROUP, own, 2 * hid), 2, rows),
        wd_part.reshape(R, deep, width),
        out_part.reshape(4, 2, length, width),
    )
    output = (mixed + out_sum).astype(BF)

    def columns(a):
        a = a[:, :own].reshape(GROUP, own, R, deep).transpose(1, 2, 0, 3)
        return a.reshape(own, R * GROUP * deep).astype(F32)

    q_sum, o_sum = q_sum[:own], o_sum[:own]
    return (
        output,
        grad_tokens,
        q_sum[:, nq + 2 * nk],
        q_sum[:, :nq],
        q_sum[:, nq : nq + nk],
        q_sum[:, nq + nk : nq + 2 * nk],
        o_sum,
        q_sum[:, nq + 2 * nk + 1],
        columns(gu_sum[:, :, :hid]),
        columns(gu_sum[:, :, hid:]),
        wd_sum,
    )


def solution(mesh):
    n = mesh.shape[AXIS]
    in_specs = (
        P(AXIS, None),
        P(AXIS),
        P(AXIS, None),
        P(AXIS, None),
        P(AXIS, None),
        P(AXIS, None),
        P(AXIS),
        P(AXIS, None),
        P(AXIS, None),
        P(AXIS, None),
        P(AXIS, None),
    )
    out_specs = (
        P(AXIS, None),
        P(AXIS, None),
        P(AXIS),
        P(AXIS, None),
        P(AXIS, None),
        P(AXIS, None),
        P(AXIS, None),
        P(AXIS),
        P(AXIS, None),
        P(AXIS, None),
        P(AXIS, None),
    )
    return jax.shard_map(
        functools.partial(body, n // GROUP),
        mesh=mesh,
        in_specs=in_specs,
        out_specs=out_specs,
        check_vma=False,
    )
```
